32 devices in a mesh: dp: 32 (over z, y, x, core), tensor: 1.
Axes of the slice: x: 2, y: 2, z: 4, core: 2. Of those that a mesh axis runs over, the one named last changes fastest.
Arguments:
- activations: bfloat16 [8192, 14336], P('dp', 'tensor'), may hold values from -6 to 6
- out_grads: bfloat16 [8192, 4096], P('dp', 'tensor'), may hold values from -0.06591797 to 0.06591797
Outputs:
- fisher: float32 [14336, 4096], P('tensor', 'dp')
The draws below stay inside these ranges and needn't reach their ends.
All inputs are finite; a program needn't handle non-finite values.
Results may differ from the reference program's by a relative error of at most 0.0003.
Values may be sent and summed in bfloat16 or wider, within the bound.
A program may use at most 896 MiB of HBM per device.

```python
import jax
import jax.numpy as jnp
from jax import lax

FF = 14336
D = 4096
LEN = 128
SEQ_DEV = 2
SEQS = 64
TOKENS = 8192
N_DP = 32


def spiked(result, rng, source, target, shards_of, factor):
    def block_of(dim):
        return (jnp.arange(result.shape[dim]) // (result.shape[dim] // shards_of)).reshape((-1,) + (1,) * (result.ndim - 1 - dim))

    first = jax.random.permutation(rng, shards_of)[block_of(target)]
    far = (block_of(target) + shards_of // 2) % shards_of
    return jnp.where((block_of(source) == first) | (block_of(source) == far), factor * result, result)


def level_of(own_key, extent, split, least, top_value):
    level = 1.0
    for position, blocks in split:
        heights = jax.random.uniform(jax.random.fold_in(jax.random.fold_in(own_key, 6), position), (blocks,), jnp.float32, least / len(split), top_value / len(split))
        level = level * jnp.repeat(jnp.exp(heights), extent[position] // blocks).reshape((-1,) + (1,) * (len(extent) - 1 - position))
    return level


def centred(key, shape, scale, reach, split=(), held_as=jnp.bfloat16):
    drawn = scale * jax.random.normal(key, shape, jnp.float32)
    if split:
        drawn = drawn * level_of(key, shape, split, -0.22, 0.18)
    return jnp.clip(drawn, -reach, reach).astype(held_as)


def gaussian_with(key, extent, deviation, limit, cuts, heavy, held_as=jnp.bfloat16):
    entries = deviation * jax.random.normal(key, extent, jnp.float32)
    if cuts:
        entries = entries * level_of(key, extent, cuts, -0.22, 0.18)
    return jnp.clip(spiked(entries, jax.random.fold_in(key, 3), *heavy), -limit, limit).astype(held_as)


def setup_inputs(seed: int = 0) -> dict:
    key_list = jax.random.split(jax.random.key(seed), 3)
    return {
        "activations": centred(key_list[0], (TOKENS, FF), 1.0, 6.0, ((0, 32),)),
        "out_grads": gaussian_with(key_list[1], (TOKENS, D), ((LEN * SEQS) ** -0.5), 0.06591797, ((0, 32),), (0, 1, 32, 2.75)),
    }


def group_partial(inputs_group, grads_group):
    def add_sequence(total, pair):
        grads = jnp.dot(pair[0].T, pair[1], preferred_element_type=jnp.float32)
        return total + grads * grads, None

    start = jnp.zeros((FF, D), jnp.float32)
    total, unused = lax.scan(add_sequence, start, (inputs_group, grads_group))
    return total


def reference(activations, out_grads):
    inputs_all = activations.reshape(N_DP, SEQ_DEV, LEN, FF)
    grads_all = out_grads.reshape(N_DP, SEQ_DEV, LEN, D)

    def add_group(fisher, pair):
        return fisher + group_partial(pair[0], pair[1]), None

    fisher, unused = lax.scan(add_group, jnp.zeros((FF, D), jnp.float32), (inputs_all, grads_all))
    return fisher
```

```python
import functools

import jax
import jax.numpy as jnp
from jax import lax
from jax.experimental import pallas as pl
from jax.experimental.pallas import tpu as pltpu
from jax.sharding import PartitionSpec as P

LEN = 128
TILE_F = 256
TILE_D = 512
VMEM_BYTES = 48 * 1024 * 1024


def squares_kernel(near_ref, far_ref, grads_ref, out_ref, turned):
    seqs = near_ref.shape[0]
    tile_d = out_ref.shape[0] * out_ref.shape[2]
    owned = out_ref.shape[2]

    @pl.when(pl.program_id(1) == 0)
    def turn():
        for s in range(seqs):
            turned[2 * s] = near_ref[s].T
            turned[2 * s + 1] = far_ref[s].T

    start = pl.multiple_of(pl.program_id(1) * tile_d, tile_d)
    for half in range(tile_d // 256):
        total = jnp.zeros((turned.shape[1], 256), jnp.float32)
        for s in range(2 * seqs):
            grads = jnp.dot(
                turned[s],
                grads_ref[s, :, pl.ds(start + half * 256, 256)],
                preferred_element_type=jnp.float32,
            )
            total = total + grads * grads
        for j in range(256 // owned):
            out_ref[half * (256 // owned) + j] = total[:, j * owned:(j + 1) * owned]


def squares(near, far, grads, owned):
    seqs, _, f = near.shape
    d = grads.shape[2]
    inputs = pl.BlockSpec((seqs, LEN, TILE_F), lambda i, j: (0, 0, i))
    return pl.pallas_call(
        squares_kernel,
        grid=(f // TILE_F, d // TILE_D),
        in_specs=[inputs, inputs, pl.BlockSpec((2 * seqs, LEN, d), lambda i, j: (0, 0, 0))],
        out_specs=pl.BlockSpec((TILE_D // owned, TILE_F, owned), lambda i, j: (j, i, 0)),
        out_shape=jax.ShapeDtypeStruct((d // owned, f, owned), jnp.float32),
        scratch_shapes=[pltpu.VMEM((2 * seqs, TILE_F, LEN), jnp.bfloat16)],
        compiler_params=pltpu.CompilerParams(vmem_limit_bytes=VMEM_BYTES),
        cost_estimate=pl.CostEstimate(
            flops=2 * 2 * seqs * LEN * f * d,
            bytes_accessed=2 * 2 * seqs * LEN * (f + d) + 4 * f * d,
            transcendentals=0,
        ),
    )(near, far, grads)


def scattered(activations, gathered, n):
    seqs, f = activations.shape[0] // LEN, activations.shape[1]
    a = activations.reshape(seqs, LEN, f)
    g = gathered.reshape(seqs, LEN, gathered.shape[1])
    total = 0.0
    for s in range(seqs):
        grads = jnp.dot(g[s].T, a[s], preferred_element_type=jnp.float32)
        total = total + grads * grads
    return lax.psum_scatter(total, "dp", scatter_dimension=0, tiled=True).T


def per_device(n, activations, out_grads):
    gathered = lax.all_gather(out_grads, "tensor", axis=1, tiled=True)
    rows, f = activations.shape
    d = gathered.shape[1]
    owned = d // n
    inner, lo = 8, 2
    hi = n // (inner * lo)
    tiles = f // (inner * TILE_F)
    if n % (inner * lo) or f % (inner * TILE_F) or owned != 128:
        return scattered(activations, gathered, n)

    me = lax.axis_index("dp")
    h, l = me // (inner * lo), (me // inner) % lo
    groups = [[k * inner + i for i in range(inner)] for k in range(n // inner)]
    swap_lo = [(k, k ^ inner) for k in range(n)]
    step = inner * lo

    with jax.named_scope("grads_exchange"):
        g = gathered.reshape(rows, hi, lo, inner * owned)
        mine = lax.dynamic_index_in_dim(g, l, 2, keepdims=False)
        theirs = lax.dynamic_index_in_dim(g, 1 - l, 2, keepdims=False)
        got = lax.ppermute(theirs, "dp", swap_lo)
        both = jnp.stack([mine, got])
        seqs = rows // LEN
        cols = []
        for shift in list(range(1, hi)) + [0]:
            part = lax.dynamic_index_in_dim(both, (h + shift) % hi, 2, keepdims=False)
            part = part.reshape(2, seqs, LEN, inner * owned).transpose(1, 0, 2, 3)
            part = lax.all_gather(part, "dp", axis_index_groups=groups)
            cols.append(part.reshape(inner * seqs * 2, LEN, inner * owned))

    sizes = [1] + [2] * ((tiles - 1) // 2) + [1] * ((tiles - 1) % 2)
    wide = f // inner
    a = activations.reshape(rows, inner, wide)
    pieces = []
    first = 0
    for size in sizes:
        chunk = a[:, :, first * TILE_F:(first + size) * TILE_F].transpose(1, 0, 2)
        first += size
        with jax.named_scope("inputs_exchange"):
            near = lax.all_to_all(chunk, "dp", 0, 0, axis_index_groups=groups, tiled=True)
            near = near.reshape(inner * seqs, LEN, size * TILE_F)
            far = lax.ppermute(near, "dp", swap_lo)
        arrived = []
        for shift in range(1, hi):
            part = squares(near, far, cols[shift - 1], owned)
            pairs = [(k, (k + shift * step) % n) for k in range(n)]
            arrived.append(lax.ppermute(part, "dp", pairs))
        total = squares(near, far, cols[-1], owned)
        for part in arrived:
            total = total + part
        with jax.named_scope("to_owners"):
            pieces.append(lax.all_to_all(total, "dp", 0, 0, axis_index_groups=groups, tiled=True))
    return jnp.concatenate(pieces, axis=1).reshape(f, owned)


def solution(mesh):
    in_specs = (P("dp", "tensor"), P("dp", "tensor"))
    out_specs = P("tensor", "dp")
    body = functools.partial(per_device, mesh.shape["dp"])
    return jax.shard_map(
        body, mesh=mesh, in_specs=in_specs, out_specs=out_specs, check_vma=False
    )
```

```python
import functools

import jax
import jax.numpy as jnp
from jax import lax
from jax.experimental import pallas as pl
from jax.experimental.pallas import tpu as pltpu
from jax.sharding import PartitionSpec as P

LEN = 128
TILE_F = 256
TILE_D = 512
VMEM_BYTES = 48 * 1024 * 1024


def squares_kernel(per, near_ref, far_ref, grads_ref, *refs):
    out_ref, turned = refs[-2:]
    seqs = near_ref.shape[0]
    chips = seqs // (2 * per)
    tile_d = out_ref.shape[0] * out_ref.shape[2]
    owned = out_ref.shape[2]

    @pl.when(pl.program_id(1) == 0)
    def turn():
        for core in range(2):
            for chip in range(chips):
                for s in range(per):
                    source = (chip * 2 + core) * per + s
                    place = (core * chips + chip) * 2 * per + s
                    turned[place] = near_ref[source].T
                    turned[place + per] = far_ref[source].T

    start = pl.multiple_of(pl.program_id(1) * tile_d, tile_d)
    for half in range(tile_d // 256):
        total = jnp.zeros((turned.shape[1], 256), jnp.float32)
        for s in range(2 * seqs):
            grads = jnp.dot(
                turned[s],
                grads_ref[s, :, pl.ds(start + half * 256, 256)],
                preferred_element_type=jnp.float32,
            )
            total = total + grads * grads
        for j in range(256 // owned):
            out_ref[half * (256 // owned) + j] = total[:, j * owned:(j + 1) * owned]


def squares(per, near, far, grads, owned, after):
    seqs, _, f = near.shape
    d = grads.shape[2]
    inputs = pl.BlockSpec((seqs, LEN, TILE_F), lambda i, j: (0, 0, i))
    return pl.pallas_call(
        functools.partial(squares_kernel, per),
        grid=(f // TILE_F, d // TILE_D),
        in_specs=[inputs, inputs, pl.BlockSpec((2 * seqs, LEN, d), lambda i, j: (0, 0, 0))]
        + [pl.BlockSpec(memory_space=pl.ANY)] * len(after),
        out_specs=pl.BlockSpec((TILE_D // owned, TILE_F, owned), lambda i, j: (j, i, 0)),
        out_shape=jax.ShapeDtypeStruct((d // owned, f, owned), jnp.float32),
        scratch_shapes=[pltpu.VMEM((2 * seqs, TILE_F, LEN), jnp.bfloat16)],
        compiler_params=pltpu.CompilerParams(vmem_limit_bytes=VMEM_BYTES),
        cost_estimate=pl.CostEstimate(
            flops=2 * 2 * seqs * LEN * f * d,
            bytes_accessed=2 * 2 * seqs * LEN * (f + d) + 4 * f * d,
            transcendentals=0,
        ),
    )(near, far, grads, *after)


def scattered(activations, gathered, n):
    seqs, f = activations.shape[0] // LEN, activations.shape[1]
    a = activations.reshape(seqs, LEN, f)
    g = gathered.reshape(seqs, LEN, gathered.shape[1])
    total = 0.0
    for s in range(seqs):
        grads = jnp.dot(g[s].T, a[s], preferred_element_type=jnp.float32)
        total = total + grads * grads
    return lax.psum_scatter(total, "dp", scatter_dimension=0, tiled=True).T


def per_device(n, activations, out_grads):
    gathered = lax.all_gather(out_grads, "tensor", axis=1, tiled=True)
    rows, f = activations.shape
    d = gathered.shape[1]
    owned = d // n
    inner, lo = 8, 2
    hi = n // (inner * lo)
    tiles = f // (inner * TILE_F)
    if n % (inner * lo) or hi < 2 or tiles < 3 or f % (inner * TILE_F) or owned != 128:
        return scattered(activations, gathered, n)

    me = lax.axis_index("dp")
    h, l = me // (inner * lo), (me // inner) % lo
    groups = [[k * inner + i for i in range(inner)] for k in range(n // inner)]
    chips = [[k * inner + 2 * q + c for q in range(inner // 2)] for k in range(n // inner) for c in range(2)]
    cores = [[2 * k, 2 * k + 1] for k in range(n // 2)]
    swap_lo = [(k, k ^ inner) for k in range(n)]
    step = inner * lo

    with jax.named_scope("grads_exchange"):
        g = gathered.reshape(rows, hi, lo, inner * owned)
        mine = lax.dynamic_index_in_dim(g, l, 2, keepdims=False)
        theirs = lax.dynamic_index_in_dim(g, 1 - l, 2, keepdims=False)
        got = lax.ppermute(theirs, "dp", swap_lo)
        both = jnp.stack([mine, got])
        seqs = rows // LEN
        cols = []
        for shift in list(range(1, hi)) + [0]:
            part = lax.dynamic_index_in_dim(both, (h + shift) % hi, 2, keepdims=False)
            part = part.reshape(2 * seqs, LEN, inner * owned)
            part = lax.all_gather(part, "dp", axis_index_groups=chips, tiled=True)
            part = lax.all_gather(part, "dp", axis_index_groups=cores, tiled=True)
            cols.append(part.reshape(inner * seqs * 2, LEN, inner * owned))

    sizes = [1] + [2] * ((tiles - 3) // 2) + [1] * (tiles - 1 - 2 * ((tiles - 3) // 2))
    wide = f // inner
    a = activations.reshape(rows, inner, wide)
    sources = []
    first = 0
    for size in sizes:
        chunk = a[:, :, first * TILE_F:(first + size) * TILE_F].transpose(1, 0, 2)
        first += size
        with jax.named_scope("inputs_exchange"):
            near = lax.all_to_all(chunk, "dp", 0, 0, axis_index_groups=groups, tiled=True)
            near = near.reshape(inner * seqs, LEN, size * TILE_F)
            far = lax.ppermute(near, "dp", swap_lo)
        sources.append((near, far))

    sent, arrived = [], []
    for near, far in sources:
        landed = []
        for shift in range(1, hi):
            part = squares(seqs, near, far, cols[shift - 1], owned, sent[-1:])
            pairs = [(k, (k + shift * step) % n) for k in range(n)]
            sent.append(part)
            landed.append(lax.ppermute(part, "dp", pairs))
        arrived.append(landed)
    pieces, total = [], None
    for k, (near, far) in enumerate(sources):
        after = [sent[min(k + 2, len(sources) - 1) * (hi - 1)]]
        after += ([total] if k >= 1 else []) + ([pieces[k - 2]] if k >= 2 else [])
        total = squares(seqs, near, far, cols[-1], owned, after)
        for part in arrived[k]:
            total = total + part
        with jax.named_scope("to_owners"):
            pieces.append(lax.all_to_all(total, "dp", 0, 0, axis_index_groups=groups, tiled=True))
    return jnp.concatenate(pieces, axis=1).reshape(f, owned)


def solution(mesh):
    in_specs = (P("dp", "tensor"), P("dp", "tensor"))
    out_specs = P("tensor", "dp")
    body = functools.partial(per_device, mesh.shape["dp"])
    return jax.shard_map(
        body, mesh=mesh, in_specs=in_specs, out_specs=out_specs, check_vma=False
    )
```
